1024 devices in a mesh: blk: 128 (over z_lo, x, y), grp: 8 (over z_hi, core).
Axes of the slice: x: 4, y: 8, z: 16 (z_hi: 4, z_lo: 4; z = z_hi * 4 + z_lo), core: 2. Of those that a mesh axis runs over, the one named last changes fastest.
Arguments:
- image_emb: float32 [262144, 768], P(('blk', 'grp')), may hold values from -0.25 to 0.25
- text_emb: float32 [262144, 768], P(('blk', 'grp')), may hold values from -0.25 to 0.25
- labels: int32 [262144], P(('blk', 'grp')), may hold values from 0 to 255
- logit_scale: float32 [1], replicated, may hold values from 40 to 80
- logit_bias: float32 [1], replicated, may hold values from -9 to -4
Outputs:
- image_grad: float32 [262144, 768], P(('blk', 'grp'))
- text_grad: float32 [262144, 768], P(('blk', 'grp'))
The draws below stay inside these ranges and needn't reach their ends.
All inputs are finite; a program needn't handle non-finite values.
Results may differ from the reference program's by a relative error of at most 0.0003.
Values sent between devices are 32-bit elements; how exact they have to be, the bound alone decides.
No kernel may reach another device: no remote copies, remote signals or barrier semaphores. Data moves between devices by JAX's collectives and lax.ppermute only.
A program may use at most 32 MiB of HBM per device.

```python
import jax
import jax.numpy as jnp
from jax import lax

D = 768
ROWS = 256
BATCH = 262144
N_BLK = 128
N_GRP = 8


def plant(drawn, key, smallest, high):
    shape = drawn.shape
    index_at = [jax.random.randint(jax.random.fold_in(key, axis), (), 0, shape[axis]) for axis in range(len(shape))]
    drawn = drawn.at[tuple(index_at)].set(smallest)
    longest = shape.index(max(shape))
    index_at[longest] = (index_at[longest] + 1) % shape[longest]
    return drawn.at[tuple(index_at)].set(high)


def block_scale(own_key, dims, pieces, smallest, largest):
    factor_of, own = 1.0, jax.random.fold_in(own_key, 6)
    for axis_at, blocks in pieces:
        steps = jnp.exp(jax.random.uniform(jax.random.fold_in(own, axis_at), (blocks,), jnp.float32, smallest / len(pieces), largest / len(pieces)))
        factor_of = factor_of * jnp.repeat(steps, dims[axis_at] // blocks).reshape([-1 if axis == axis_at else 1 for axis in range(len(dims))])
    return factor_of


def centred(own_key, shape, deviation, most, shards=(), held_as=jnp.bfloat16):
    array = deviation * jax.random.normal(own_key, shape, jnp.float32)
    if shards:
        array = array * block_scale(own_key, shape, shards, -0.22, 0.18)
    return jnp.clip(array, -most, most).astype(held_as)


def setup_inputs(seed: int = 0) -> dict:
    arg_keys = jax.random.split(jax.random.key(seed), 6)
    image_emb = centred(arg_keys[0], (BATCH, D), 0.036, 0.25, ((0, 1024),), jnp.float32)
    text_emb = centred(arg_keys[1], (BATCH, D), 0.036, 0.25, ((0, 1024),), jnp.float32)
    labels = plant(jax.random.randint(arg_keys[2], (BATCH,), 0, ROWS), jax.random.fold_in(arg_keys[2], 1), 0, ROWS - 1).astype(jnp.int32)
    logit_scale = jnp.clip(jax.random.uniform(arg_keys[3], (1,), jnp.float32, 40.0, 80.0), 40.0, 80.0)
    logit_bias = jnp.clip(jax.random.uniform(arg_keys[4], (1,), jnp.float32, -9.0, -4.0), -9.0, -4.0)
    return dict(image_emb=image_emb, text_emb=text_emb, labels=labels, logit_scale=logit_scale, logit_bias=logit_bias)


EPS = 1e-06
HIGH = lax.Precision.HIGHEST

def unit_rows(rows):
    return rows * lax.rsqrt(lax.optimization_barrier(jnp.sum(rows * rows, -1, keepdims=True)) + EPS)

def norm_backward(rows, grad):
    inverse = lax.rsqrt(lax.optimization_barrier(jnp.sum(rows * rows, -1, keepdims=True)) + EPS)
    unit = rows * inverse
    return inverse * (grad - unit * lax.optimization_barrier(jnp.sum(unit * grad, -1, keepdims=True)))

def reference(image_emb, text_emb, labels, logit_scale, logit_bias):
    scale = logit_scale[0]
    bias = logit_bias[0]
    images = image_emb.reshape(N_BLK, N_GRP, ROWS, D)
    texts = text_emb.reshape(N_BLK, N_GRP, ROWS, D)
    marks = labels.reshape(N_BLK, N_GRP, ROWS)
    half_blk = N_BLK // 2
    half_grp = N_GRP // 2
    columns = jnp.arange(ROWS, dtype=jnp.int32)
    own_slot = (jnp.arange(4, dtype=jnp.int32) == 0).astype(jnp.float32)[None, :, None, None]

    def partners(near, far_rows):
        return jnp.stack([near, jnp.roll(near, -half_grp, 0), far_rows, jnp.roll(far_rows, -half_grp, 0)], 1)

    def per_block(index):
        far = (index + half_blk) % N_BLK
        image_near = unit_rows(images[index])
        image_far = unit_rows(images[far])
        text_near = unit_rows(texts[index])
        text_far = unit_rows(texts[far])
        text_sets = partners(text_near, text_far)
        image_sets = partners(image_near, image_far)
        positive = (marks[index][:, :, None] == columns[None, None, :]).astype(jnp.float32)[:, None] * own_slot
        logits = scale * jnp.einsum('grd,gmcd->gmrc', image_near, text_sets, precision=HIGH) + bias
        slope = jax.nn.sigmoid(logits) - positive
        grad_image = scale * jnp.einsum('gmrc,gmcd->grd', slope, text_sets, precision=HIGH)
        back_logits = scale * jnp.einsum('gmrd,gcd->gmrc', image_sets, text_near, precision=HIGH) + bias
        back_slope = jax.nn.sigmoid(back_logits) - positive
        grad_text = scale * jnp.einsum('gmrc,gmrd->gcd', back_slope, image_sets, precision=HIGH)
        return (norm_backward(images[index], grad_image), norm_backward(texts[index], grad_text))
    image_grad, text_grad = lax.map(per_block, jnp.arange(N_BLK, dtype=jnp.int32))
    return (image_grad.reshape(image_emb.shape), text_grad.reshape(text_emb.shape))
```

```python
import jax
import jax.numpy as jnp
from jax import lax
from jax.sharding import PartitionSpec as P

EPS = 1e-06
HIGH = lax.Precision.HIGHEST
AXES = ("blk", "grp")
CHUNKS = 4


def exchanged(value, flip):
    size = lax.axis_size("blk") * lax.axis_size("grp")
    return lax.ppermute(value, AXES, [(source, source ^ flip) for source in range(size)])


def unit_rows(rows):
    return rows * lax.rsqrt(jnp.sum(rows * rows, -1, keepdims=True) + EPS)


def norm_backward(rows, grad):
    inverse = lax.rsqrt(jnp.sum(rows * rows, -1, keepdims=True) + EPS)
    unit = rows * inverse
    return inverse * (grad - unit * jnp.sum(unit * grad, -1, keepdims=True))


def shards(image_emb, text_emb, labels, logit_scale, logit_bias):
    scale = logit_scale[0]
    bias = logit_bias[0]
    rows = image_emb.shape[0]
    n_grp = lax.axis_size("grp")
    near = (lax.axis_size("blk") // 2) * n_grp
    far = near + n_grp // 2
    part = rows // CHUNKS

    far_images = [exchanged(image_emb[i * part:(i + 1) * part], far) for i in range(CHUNKS)]
    near_text = exchanged(text_emb, near)

    texts = jnp.concatenate([unit_rows(text_emb), unit_rows(near_text)], 0)
    columns = jnp.arange(2 * rows, dtype=jnp.int32)

    def tile(images, marks):
        logits = scale * jnp.einsum("rd,cd->rc", images, texts, precision=HIGH) + bias
        slope = jax.nn.sigmoid(logits)
        if marks is not None:
            slope = slope - (marks[:, None] == columns[None, :]).astype(jnp.float32)
        grad_image = scale * jnp.einsum("rc,cd->rd", slope, texts, precision=HIGH)
        grad_text = scale * jnp.einsum("rc,rd->cd", slope, images, precision=HIGH)
        return grad_image, grad_text

    own_image_grad, text_grads = tile(unit_rows(image_emb), labels)
    returned = []
    for chunk in far_images:
        grad_image, grad_text = tile(unit_rows(chunk), None)
        returned.append(exchanged(grad_image, far))
        text_grads = text_grads + grad_text
    near_back = exchanged(text_grads[rows:], near)
    grad_image = own_image_grad + jnp.concatenate(returned, 0)
    grad_text = text_grads[:rows] + near_back
    return (norm_backward(image_emb, grad_image), norm_backward(text_emb, grad_text))


def solution(mesh):
    in_specs = (P(("blk", "grp"), None), P(("blk", "grp"), None), P(("blk", "grp")), P(), P())
    out_specs = (P(("blk", "grp"), None), P(("blk", "grp"), None))
    return jax.shard_map(shards, mesh=mesh, in_specs=in_specs, out_specs=out_specs, check_vma=False)
```

```python
import jax
import jax.numpy as jnp
from jax import lax
from jax.sharding import PartitionSpec as P

EPS = 1e-06
HIGH = lax.Precision.HIGHEST
AXES = ("blk", "grp")


def exchanged(value, flip):
    size = lax.axis_size("blk") * lax.axis_size("grp")
    return lax.ppermute(value, AXES, [(source, source ^ flip) for source in range(size)])


def unit_rows(rows):
    return rows * lax.rsqrt(jnp.sum(rows * rows, -1, keepdims=True) + EPS)


def norm_backward(rows, grad):
    inverse = lax.rsqrt(jnp.sum(rows * rows, -1, keepdims=True) + EPS)
    unit = rows * inverse
    return inverse * (grad - unit * jnp.sum(unit * grad, -1, keepdims=True))


def times(a, b):
    return jnp.einsum("rc,cd->rd", a, b, precision=HIGH)


def times_transposed(a, b):
    return jnp.einsum("rc,rd->cd", a, b, precision=HIGH)


def shards(image_emb, text_emb, labels, logit_scale, logit_bias):
    scale = logit_scale[0]
    bias = logit_bias[0]
    rows = image_emb.shape[0]
    n_grp = lax.axis_size("grp")
    near = (lax.axis_size("blk") // 2) * n_grp
    far = near + n_grp // 2

    def slopes(images, texts):
        return jax.nn.sigmoid(scale * jnp.einsum("rd,cd->rc", images, texts, precision=HIGH) + bias)

    near_emb = exchanged(text_emb, near)
    far_emb = exchanged(image_emb, far)

    image, text = unit_rows(image_emb), unit_rows(text_emb)
    columns = jnp.arange(rows, dtype=jnp.int32)
    slope = slopes(image, text) - (labels[:, None] == columns[None, :]).astype(jnp.float32)
    image_grad = times(slope, text)
    text_grad = times_transposed(slope, image)

    near_text = unit_rows(near_emb)
    slope = slopes(image, near_text)
    image_grad = image_grad + times(slope, near_text)
    near_grad = times_transposed(slope, image)
    image_grad, text_grad, near_grad, near_text = lax.optimization_barrier((image_grad, text_grad, near_grad, near_text))

    far_image = unit_rows(far_emb)
    texts = jnp.concatenate([text, near_text], 0)
    slope = slopes(far_image, texts)
    far_grad, slope = lax.optimization_barrier((scale * times(slope, texts), slope))
    far_back = exchanged(far_grad, far)
    near_back = exchanged(scale * (near_grad + times_transposed(slope[:, rows:], far_image)), near)
    text_grad = scale * (text_grad + times_transposed(slope[:, :rows], far_image))
    return (norm_backward(image_emb, scale * image_grad + far_back), norm_backward(text_emb, text_grad + near_back))


def solution(mesh):
    in_specs = (P(("blk", "grp"), None), P(("blk", "grp"), None), P(("blk", "grp")), P(), P())
    out_specs = (P(("blk", "grp"), None), P(("blk", "grp"), None))
    return jax.shard_map(shards, mesh=mesh, in_specs=in_specs, out_specs=out_specs, check_vma=False)
```

```python
import jax
import jax.numpy as jnp
from jax import lax
from jax.sharding import PartitionSpec as P

EPS = 1e-06
HIGH = lax.Precision.HIGH
AXES = ("blk", "grp")


def exchanged(value, flip):
    size = lax.axis_size("blk") * lax.axis_size("grp")
    return lax.ppermute(value, AXES, [(source, source ^ flip) for source in range(size)])


def unit_rows(rows):
    return rows * lax.rsqrt(jnp.sum(rows * rows, -1, keepdims=True) + EPS)


def norm_backward(rows, grad):
    inverse = lax.rsqrt(jnp.sum(rows * rows, -1, keepdims=True) + EPS)
    unit = rows * inverse
    return inverse * (grad - unit * jnp.sum(unit * grad, -1, keepdims=True))


def times(a, b):
    return jnp.einsum("rc,cd->rd", a, b, precision=HIGH)


def times_transposed(a, b):
    return jnp.einsum("rc,rd->cd", a, b, precision=HIGH)


def shards(image_emb, text_emb, labels, logit_scale, logit_bias):
    scale = logit_scale[0]
    bias = logit_bias[0]
    rows = image_emb.shape[0]
    n_grp = lax.axis_size("grp")
    near = (lax.axis_size("blk") // 2) * n_grp
    far = near + n_grp // 2

    def slopes(images, texts):
        return jax.nn.sigmoid(scale * jnp.einsum("rd,cd->rc", images, texts, precision=HIGH) + bias)

    near_emb = exchanged(text_emb, near)
    far_emb = exchanged(image_emb, far)

    image, text = unit_rows(image_emb), unit_rows(text_emb)
    columns = jnp.arange(rows, dtype=jnp.int32)
    slope = slopes(image, text) - (labels[:, None] == columns[None, :]).astype(jnp.float32)
    image_grad = times(slope, text)
    text_grad = times_transposed(slope, image)

    near_text = unit_rows(near_emb)
    slope = slopes(image, near_text)
    image_grad = image_grad + times(slope, near_text)
    near_grad = times_transposed(slope, image)
    image_grad, text_grad, near_grad, near_text = lax.optimization_barrier((image_grad, text_grad, near_grad, near_text))

    far_image = unit_rows(far_emb)
    texts = jnp.concatenate([text, near_text], 0)
    slope = slopes(far_image, texts)
    far_grad, slope = lax.optimization_barrier((scale * times(slope, texts), slope))
    far_back = exchanged(far_grad, far)
    near_back = exchanged(scale * (near_grad + times_transposed(slope[:, rows:], far_image)), near)
    text_grad = scale * (text_grad + times_transposed(slope[:, :rows], far_image))
    image_out = norm_backward(image_emb, scale * image_grad + far_back)
    image_out, text_grad = lax.optimization_barrier((image_out, text_grad))
    return image_out, norm_backward(text_emb, text_grad + near_back)


def solution(mesh):
    in_specs = (P(("blk", "grp"), None), P(("blk", "grp"), None), P(("blk", "grp")), P(), P())
    out_specs = (P(("blk", "grp"), None), P(("blk", "grp"), None))
    return jax.shard_map(shards, mesh=mesh, in_specs=in_specs, out_specs=out_specs, check_vma=False)
```

```python
import jax
import jax.numpy as jnp
from jax import lax
from jax.sharding import PartitionSpec as P

EPS = 1e-06
HIGH = lax.Precision.HIGH
AXES = ("blk", "grp")


def exchanged(far_value, near_value, far, near):
    size = lax.axis_size("blk") * lax.axis_size("grp")
    even = lax.axis_index("grp") % 2 == 0

    def permuted(value, even_flip, odd_flip):
        return lax.ppermute(value, AXES, [(source, source ^ (odd_flip if source % 2 else even_flip)) for source in range(size)])

    values = jnp.where(even, far_value, near_value), jnp.where(even, near_value, far_value)
    *values, far_value, near_value = lax.optimization_barrier((*values, far_value, near_value))
    first = permuted(values[0], far, near)
    second = permuted(values[1], near, far)
    return far_value, near_value, jnp.where(even, first, second), jnp.where(even, second, first)


def unit_rows(rows):
    return rows * lax.rsqrt(jnp.sum(rows * rows, -1, keepdims=True) + EPS)


def norm_backward(rows, grad):
    inverse = lax.rsqrt(jnp.sum(rows * rows, -1, keepdims=True) + EPS)
    unit = rows * inverse
    return inverse * (grad - unit * jnp.sum(unit * grad, -1, keepdims=True))


def times(a, b):
    return jnp.einsum("rc,cd->rd", a, b, precision=HIGH)


def times_transposed(a, b):
    return jnp.einsum("rc,rd->cd", a, b, precision=HIGH)


def shards(image_emb, text_emb, labels, logit_scale, logit_bias):
    scale = logit_scale[0]
    bias = logit_bias[0]
    rows = image_emb.shape[0]
    n_grp = lax.axis_size("grp")
    near = (lax.axis_size("blk") // 2) * n_grp
    far = near + n_grp // 2

    def slopes(images, texts):
        return jax.nn.sigmoid(scale * jnp.einsum("rd,cd->rc", images, texts, precision=HIGH) + bias)

    image_emb, text_emb, far_emb, near_emb = exchanged(image_emb, text_emb, far, near)

    image, text = unit_rows(image_emb), unit_rows(text_emb)
    columns = jnp.arange(rows, dtype=jnp.int32)
    slope = slopes(image, text) - (labels[:, None] == columns[None, :]).astype(jnp.float32)
    image_grad = times(slope, text)
    text_grad = times_transposed(slope, image)

    near_text = unit_rows(near_emb)
    far_image = unit_rows(far_emb)
    slope = slopes(image, near_text)
    image_grad = image_grad + times(slope, near_text)
    near_grad = times_transposed(slope, image)

    texts = jnp.concatenate([text, near_text], 0)
    slope = slopes(far_image, texts)
    far_grad = scale * times(slope, texts)
    near_grad = scale * (near_grad + times_transposed(slope[:, rows:], far_image))
    _, _, far_back, near_back = exchanged(far_grad, near_grad, far, near)
    text_grad = scale * (text_grad + times_transposed(slope[:, :rows], far_image))
    return norm_backward(image_emb, scale * image_grad + far_back), norm_backward(text_emb, text_grad + near_back)


def solution(mesh):
    in_specs = (P(("blk", "grp"), None), P(("blk", "grp"), None), P(("blk", "grp")), P(), P())
    out_specs = (P(("blk", "grp"), None), P(("blk", "grp"), None))
    return jax.shard_map(shards, mesh=mesh, in_specs=in_specs, out_specs=out_specs, check_vma=False)
```

```python
import jax
import jax.numpy as jnp
from jax import lax
from jax.sharding import PartitionSpec as P

EPS = 1e-06
HIGH = lax.Precision.HIGH
AXES = ("blk", "grp")


def permuted(value, even_flip, odd_flip):
    size = lax.axis_size("blk") * lax.axis_size("grp")
    return lax.ppermute(value, AXES, [(source, source ^ (odd_flip if source % 2 else even_flip)) for source in range(size)])


def unit_rows(rows):
    return rows * lax.rsqrt(jnp.sum(rows * rows, -1, keepdims=True) + EPS)


def norm_backward(rows, grad):
    inverse = lax.rsqrt(jnp.sum(rows * rows, -1, keepdims=True) + EPS)
    unit = rows * inverse
    return inverse * (grad - unit * jnp.sum(unit * grad, -1, keepdims=True))


def times(a, b):
    return jnp.einsum("rc,cd->rd", a, b, precision=HIGH)


def times_transposed(a, b):
    return jnp.einsum("rc,rd->cd", a, b, precision=HIGH)


def shards(image_emb, text_emb, labels, logit_scale, logit_bias):
    scale = logit_scale[0]
    bias = logit_bias[0]
    rows = image_emb.shape[0]
    n_grp = lax.axis_size("grp")
    near = (lax.axis_size("blk") // 2) * n_grp
    far = near + n_grp // 2

    def slopes(images, texts):
        return jax.nn.sigmoid(scale * jnp.einsum("rd,cd->rc", images, texts, precision=HIGH) + bias)

    odd = lax.axis_index("grp") % 2 == 1
    sent = jnp.where(odd, image_emb, text_emb), jnp.where(odd, text_emb, image_emb)
    *sent, image_emb, text_emb = lax.optimization_barrier((*sent, image_emb, text_emb))
    first = permuted(sent[0], near, far)
    second = permuted(sent[1], far, near)
    near_emb, far_emb = jnp.where(odd, second, first), jnp.where(odd, first, second)

    image, text = unit_rows(image_emb), unit_rows(text_emb)
    columns = jnp.arange(rows, dtype=jnp.int32)
    slope = slopes(image, text) - (labels[:, None] == columns[None, :]).astype(jnp.float32)
    image_grad = times(slope, text)
    text_grad = times_transposed(slope, image)

    near_text = unit_rows(near_emb)
    far_image = unit_rows(far_emb)
    slope = slopes(image, near_text)
    image_grad = image_grad + times(slope, near_text)
    near_grad = times_transposed(slope, image)

    texts = jnp.concatenate([text, near_text], 0)
    slope = slopes(far_image, texts)
    far_grad = scale * times(slope, texts)
    near_grad = scale * (near_grad + times_transposed(slope[:, rows:], far_image))
    far_back = permuted(far_grad, far, far)
    near_back = permuted(near_grad, near, near)
    text_grad = scale * (text_grad + times_transposed(slope[:, :rows], far_image))
    text_out = norm_backward(text_emb, text_grad + near_back)
    text_out, image_grad = lax.optimization_barrier((text_out, scale * image_grad))
    return norm_backward(image_emb, image_grad + far_back), text_out


def solution(mesh):
    in_specs = (P(("blk", "grp"), None), P(("blk", "grp"), None), P(("blk", "grp")), P(), P())
    out_specs = (P(("blk", "grp"), None), P(("blk", "grp"), None))
    return jax.shard_map(shards, mesh=mesh, in_specs=in_specs, out_specs=out_specs, check_vma=False)
```

```python
import jax
import jax.numpy as jnp
from jax import lax
from jax.sharding import PartitionSpec as P

EPS = 1e-06
HIGH = lax.Precision.HIGH
AXES = ("blk", "grp")


def exchanged(value, flip):
    size = lax.axis_size("blk") * lax.axis_size("grp")
    return lax.ppermute(value, AXES, [(source, source ^ flip) for source in range(size)])


def unit_rows(rows):
    return rows * lax.rsqrt(jnp.sum(rows * rows, -1, keepdims=True) + EPS)


def norm_backward(rows, grad):
    inverse = lax.rsqrt(jnp.sum(rows * rows, -1, keepdims=True) + EPS)
    unit = rows * inverse
    return inverse * (grad - unit * jnp.sum(unit * grad, -1, keepdims=True))


def times(a, b):
    return jnp.einsum("rc,cd->rd", a, b, precision=HIGH)


def times_transposed(a, b):
    return jnp.einsum("rc,rd->cd", a, b, precision=HIGH)


def shards(image_emb, text_emb, labels, logit_scale, logit_bias):
    scale = logit_scale[0]
    bias = logit_bias[0]
    rows = image_emb.shape[0]
    n_grp = lax.axis_size("grp")
    near = (lax.axis_size("blk") // 2) * n_grp
    far = near + n_grp // 2

    def slopes(images, texts):
        return jax.nn.sigmoid(scale * jnp.einsum("rd,cd->rc", images, texts, precision=HIGH) + bias)

    near_emb = exchanged(text_emb, near)
    far_emb = exchanged(image_emb, far)

    image, text = unit_rows(image_emb), unit_rows(text_emb)
    columns = jnp.arange(rows, dtype=jnp.int32)
    slope = slopes(image, text) - (labels[:, None] == columns[None, :]).astype(jnp.float32)
    image_grad = times(slope, text)
    text_grad = times_transposed(slope, image)

    near_text = unit_rows(near_emb)
    slope = slopes(image, near_text)
    image_grad = image_grad + times(slope, near_text)
    near_grad = times_transposed(slope, image)
    image_grad, text_grad, near_grad, near_text = lax.optimization_barrier((image_grad, text_grad, near_grad, near_text))

    far_image = unit_rows(far_emb)
    texts = jnp.concatenate([text, near_text], 0)
    slope = slopes(far_image, texts)
    far_grad, slope = lax.optimization_barrier((scale * times(slope, texts), slope))
    far_back = exchanged(far_grad, far)
    near_back = exchanged(scale * (near_grad + times_transposed(slope[:, rows:], far_image)), near)
    text_grad = scale * (text_grad + times_transposed(slope[:, :rows], far_image))
    return (norm_backward(image_emb, scale * image_grad + far_back), norm_backward(text_emb, text_grad + near_back))


def solution(mesh):
    in_specs = (P(("blk", "grp"), None), P(("blk", "grp"), None), P(("blk", "grp")), P(), P())
    out_specs = (P(("blk", "grp"), None), P(("blk", "grp"), None))
    return jax.shard_map(shards, mesh=mesh, in_specs=in_specs, out_specs=out_specs, check_vma=False)
```
